32 devices in a mesh: groups: 2 (over x), row: 4 (over z), col: 4 (over y, core).
Axes of the slice: x: 2, y: 2, z: 4, core: 2. Of those that a mesh axis runs over, the one named last changes fastest.
Arguments:
- tokens: bfloat16 [1024, 6144], P(('groups', 'row'), 'col'), parts along dimension 0, may hold values from -6 to 6
- cotangent: bfloat16 [1024, 6144], P(('groups', 'row'), 'col'), parts along dimension 0, may hold values from -0.625 to 0.625
- up_weight: bfloat16 [6144, 24576], P('col', 'row'), may hold values from -0.078125 to 0.078125
- down_weight: bfloat16 [24576, 6144], P('row', 'col'), may hold values from -0.0390625 to 0.0390625
- up_mask: int32 [48, 192], P('col', 'row'), may hold values from 0 to 1, as said below
- down_mask: int32 [192, 48], P('row', 'col'), may hold values from 0 to 1, as said below
Outputs:
- up_grad: bfloat16 [12288, 24576], P(('groups', 'col'), 'row'), parts along dimension 0
- down_grad: bfloat16 [49152, 6144], P(('groups', 'row'), 'col'), parts along dimension 0
The draws below stay inside these ranges and needn't reach their ends.
There are 2 independent parts, one for each index of `groups`. The reference program is written for one: setup_inputs(seed, part) draws one part's arguments, and reference() takes and returns one part's arrays. A program takes and returns all parts, laid end to end along the dimension named above; an argument that names none is the same for every part. Nothing has to cross between parts.
Inputs may be any that keep to these rules, and one draw needn't show every extreme that they name: `up_mask`: 1 keeps a 128 x 128 block of up_weight, 0 prunes it; the share kept differs from block row to block row and block column to block column. `down_mask`: 1 keeps a 128 x 128 block of down_weight, 0 prunes it; the share kept differs from block row to block row and block column to block column.
All inputs are finite; a program needn't handle non-finite values.
Results may differ from the reference program's by a relative error of at most 0.015.
Values may be sent and summed in bfloat16 or wider, within the bound.
No kernel may reach another device: no remote copies, remote signals or barrier semaphores. Data moves between devices by JAX's collectives and lax.ppermute only.
A program may use at most 320 MiB of HBM per device.

```python
import jax
import jax.numpy as jnp
from jax import lax

D = 6144
FF = 24576
BLOCK = 128
TOKENS = 512
N_COL = 4


def block_mask(key, count_rows, count_cols):
    first, second, third = jax.random.split(key, 3)
    row_level = jax.random.randint(first, (count_rows, 1), 5, 50)
    col_level = jax.random.randint(second, (1, count_cols), 5, 50)
    dice = jax.random.randint(third, (count_rows, count_cols), 0, 100)
    return (dice < row_level + col_level).astype(jnp.int32)


def draw_up_mask(key, part):
    key = jax.random.fold_in(key, 11)
    return block_mask(key, D // BLOCK, FF // BLOCK)


def draw_down_mask(key, part):
    key = jax.random.fold_in(key, 23)
    return block_mask(key, FF // BLOCK, D // BLOCK)


def block_scale(key, dims, pieces, least, top_value):
    def one(dim, blocks):
        heights = jax.random.uniform(jax.random.fold_in(jax.random.fold_in(key, 6), dim), (blocks,), jnp.float32, least / len(pieces), top_value / len(pieces))
        return jnp.repeat(jnp.exp(heights), dims[dim] // blocks).reshape((-1,) + (1,) * (len(dims) - dim - 1))

    gain = one(*pieces[0])
    for cut in pieces[1:]:
        gain = gain * one(*cut)
    return gain


def centred(key, extent, scale, most, cuts=(), held_as=jnp.bfloat16):
    values = jax.random.normal(key, extent, jnp.float32) * scale
    if len(cuts) > 0:
        values = block_scale(key, extent, cuts, -0.22, 0.18) * values
    return jnp.clip(values, min=-most, max=most).astype(held_as)


def setup_inputs(seed: int = 0, part: int = 0) -> dict:
    key_list = jax.random.split(jax.random.key(seed), 7)
    part_keys = jax.random.split(jax.random.fold_in(key_list[6], part), 7)
    return {
        "tokens": centred(part_keys[0], (TOKENS, D), 1.0, 6.0, ((0, 4), (1, 4))),
        "cotangent": centred(part_keys[1], (TOKENS, D), (TOKENS ** -0.5), 0.625, ((0, 4), (1, 4))),
        "up_weight": centred(key_list[2], (D, FF), D ** -0.5, 0.078125, ((0, 4), (1, 4))),
        "down_weight": centred(key_list[3], (FF, D), FF ** -0.5, 0.0390625, ((0, 4), (1, 4))),
        "up_mask": draw_up_mask(jax.random.fold_in(key_list[6], 71), part),
        "down_mask": draw_down_mask(jax.random.fold_in(key_list[6], 71), part),
    }


SQRT_HALF = 0.7071067811865476
INV_ROOT_TWO_PI = 0.3989422804014327


def expand(mask, dtype):
    return jnp.repeat(jnp.repeat(mask.astype(dtype), BLOCK, 0), BLOCK, 1)


def gelu_slope(value):
    return 0.5 * (1.0 + lax.erf(value * SQRT_HALF)) + value * jnp.exp(-0.5 * value * value) * INV_ROOT_TWO_PI


def blocked_sum(left, right):
    width = left.shape[1] // N_COL
    left_parts = left.reshape(left.shape[0], N_COL, width).transpose(1, 0, 2)
    right_parts = right.reshape(N_COL, width, right.shape[1])

    def add_part(carry, pair):
        part = jnp.dot(pair[0], pair[1], preferred_element_type=jnp.float32)
        rounded = lax.optimization_barrier(part.astype(jnp.bfloat16))
        return carry + rounded.astype(jnp.float32), None

    start = jnp.zeros((left.shape[0], right.shape[1]), jnp.float32)
    total, unused = lax.scan(add_part, start, (left_parts, right_parts))
    return total


def reference(tokens, cotangent, up_weight, down_weight, up_mask, down_mask):
    up_kept = up_weight * expand(up_mask, up_weight.dtype)
    down_kept = down_weight * expand(down_mask, down_weight.dtype)
    hidden = blocked_sum(tokens, up_kept)
    activation = jax.nn.gelu(hidden, approximate=False).astype(jnp.bfloat16)
    down_full = jnp.dot(activation.T, cotangent, preferred_element_type=jnp.float32)
    down_grad = (down_full * expand(down_mask, jnp.float32)).astype(jnp.bfloat16)
    grad_act = blocked_sum(cotangent, down_kept.T)
    grad_hidden = (grad_act * gelu_slope(hidden)).astype(jnp.bfloat16)
    up_full = jnp.dot(tokens.T, grad_hidden, preferred_element_type=jnp.float32)
    up_grad = (up_full * expand(up_mask, jnp.float32)).astype(jnp.bfloat16)
    return up_grad, down_grad
```

```python
import functools

import jax
import jax.numpy as jnp
from jax import lax
from jax.experimental import pallas as pl
from jax.experimental.pallas import tpu as pltpu
from jax.sharding import PartitionSpec as P

BLOCK = 128
CORES = 2
VMEM_BYTES = 20 * 1024 * 1024

SQRT_HALF = 0.7071067811865476
INV_ROOT_TWO_PI = 0.3989422804014327

ANY = pl.BlockSpec(memory_space=pl.ANY)
VMEM = pl.BlockSpec(memory_space=pltpu.VMEM)

TICKET = jax.ShapeDtypeStruct((8, 128), jnp.float32)

BRIEF = pl.CostEstimate(flops=10**10, bytes_accessed=0, transcendentals=0)


CUTS = {
    "h0": (2, 2, 4),
    "h0s": (2, 2, 4),
    "g0": (4, 4),
    "g0s": (4, 4),
    "h1": (2, 2, 4),
    "h1s": (2, 2, 4),
    "g1": (2, 2, 2, 1, 1),
    "g1s": (2, 2, 2, 2),
    "a": (2, 2, 4),
    "e": (2, 2, 2, 1, 1),
}

ORDER = [
    ("send", "h0s", 0),
    ("turn", "x", 0),
    ("turn", "x", 1),
    ("send", "h0s", 1),
    ("add", "h0", 0),
    ("send", "h0s", 2),
    ("add", "h0", 1),
    ("send", "g0s", 0, ("x", 1)),
    ("turn", "x", 2),
    ("add", "h0", 2),
    ("send", "g0s", 1, ("h0", 0)),
    ("add", "g0", 0),
    ("add", "g0", 1, ("x", 0)),
    ("stack", "x", 0, ("h0", 2)),
    ("turn", "c", 0),
    ("send", "h1s", 0),
    ("send", "h1s", 2),
    ("send", "h1s", 1, ("g0", 0), ("h0", 1)),
    ("add", "h1", 0),
    ("turn", "c", 2),
    ("turn", "c", 1),
    ("add", "h1", 1),
    ("add", "h1", 2, ("g0", 1)),
    ("act", "a", 0),
    ("act", "a", 1, ("c", 0)),
    ("stack", "c", 0),
    ("send", "g1s", 0),
    ("down", "a", 0),
    ("add", "g1", 0),
    ("send", "g1s", 1),
    ("down", "a", 1),
    ("add", "g1", 1),
    ("send", "g1s", 2),
    ("send", "g1s", 3),
    ("act", "a", 2),
    ("add", "g1", 2),
    ("add", "g1", 3),
    ("add", "g1", 4),
    ("down", "a", 2),
    ("hidden", "e", 0),
    ("hidden", "e", 1),
    ("up", "e", 0),
    ("up", "e", 1),
    ("hidden", "e", 2),
    ("upmine", "e", 2),
    ("upother", "e", 2),
    ("hidden", "e", 3),
    ("upmine", "e", 3),
    ("upother", "e", 3),
    ("hidden", "e", 4),
    ("upmine", "e", 4),
    ("upother", "e", 4),
]


def tile_of(extent, most, *offsets):
    return max(
        width
        for width in range(BLOCK, most + 1, BLOCK)
        if all(size % width == 0 for size in (extent, *offsets))
    )


def spread_mask(mask, down, first, units):
    bits = mask[...].astype(jnp.bfloat16)
    tall, wide = bits.shape
    if down:
        count = units // BLOCK
        at = (count, tall)
        pick = lax.broadcasted_iota(jnp.int32, at, 0) + first == lax.broadcasted_iota(jnp.int32, at, 1)
        bits = jnp.dot(pick.astype(jnp.bfloat16), bits, preferred_element_type=jnp.float32).astype(jnp.bfloat16)
        units, first = wide * BLOCK, 0
    at = (wide, units)
    pick = lax.broadcasted_iota(jnp.int32, at, 1) // BLOCK + first == lax.broadcasted_iota(jnp.int32, at, 0)
    return jnp.dot(bits, pick.astype(jnp.bfloat16), preferred_element_type=jnp.float32).astype(jnp.bfloat16)


def units_at(down, first, width):
    run = pl.ds(first, width)
    return (run, slice(None)) if down else (slice(None), run)


def project_kernel(fresh, down, summed, waits, span, start, offset, skip, tile, half, *refs):
    refs = list(refs)
    rows = refs.pop(0)
    source = refs.pop(0)
    mask = refs.pop(0) if fresh else None
    arrived = refs.pop(0) if summed else None
    refs = refs[waits:]
    out = refs.pop(0)
    kept, sems = (refs[0], refs[-1]) if fresh else (source, None)
    steps = out.shape[1] // tile
    begin = half[0] * span + start
    copies = []
    for step in range(steps if fresh else 0):
        here = pl.multiple_of(begin + step * tile, BLOCK)
        there = kept.at[units_at(down, step * tile, tile)]
        copies.append(pltpu.make_async_copy(source.at[units_at(down, here, tile)], there, sems.at[step]))
        copies[-1].start()
    inputs = rows[pl.ds(rows.shape[0] - out.shape[0], out.shape[0]), :]
    for step in range(steps):
        first = skip + step * tile
        if fresh:
            bits = spread_mask(mask, down, (begin + step * tile) // BLOCK, tile)
            copies[step].wait()
            for i in range(bits.shape[0]):
                if down:
                    at = (pl.ds(first + i * BLOCK, BLOCK), slice(None))
                else:
                    at = (pl.ds(i * BLOCK, BLOCK), pl.ds(first, tile))
                kept[at] = kept[at] * bits[i : i + 1, :]
        total = lax.dot_general(
            inputs,
            kept[units_at(down, first, tile)],
            (((1,), (1 if down else 0,)), ((), ())),
            preferred_element_type=jnp.float32,
        )
        if summed:
            total = total + arrived[:, pl.ds(offset + step * tile, tile)].astype(jnp.float32)
        out[:, pl.ds(step * tile, tile)] = total.astype(out.dtype)


def project(inputs, count, weight, mask, down, half, span, start, skip, width, arrived, before):
    fresh = mask is not None
    tile = tile_of(width, 768)
    if fresh:
        given = [inputs, pltpu.with_memory_space_constraint(weight, pltpu.HBM), mask]
        specs = [VMEM, ANY, VMEM]
    else:
        given = [inputs, pltpu.with_memory_space_constraint(weight, pltpu.VMEM)]
        specs = [VMEM, VMEM]
    if arrived:
        given.append(arrived[0])
        specs.append(VMEM)
    shapes = [jax.ShapeDtypeStruct((count, width), jnp.bfloat16)]
    if fresh:
        model = weight.shape[1 if down else 0]
        shapes.append(pltpu.VMEM((width, model) if down else (model, width), weight.dtype))
    offset = arrived[1] if arrived else 0
    return pl.pallas_call(
        functools.partial(
            project_kernel, fresh, down, bool(arrived), len(before), span, start, offset, skip, tile
        ),
        out_shape=(*shapes, TICKET),
        in_specs=[pl.BlockSpec(memory_space=pltpu.SMEM)] + specs + [ANY] * len(before),
        out_specs=(VMEM,) * len(shapes) + (ANY,),
        scratch_shapes=[pltpu.SemaphoreType.DMA((width // tile,))] if fresh else [],
        compiler_params=pltpu.CompilerParams(vmem_limit_bytes=12 * 1024 * 1024),
        cost_estimate=BRIEF,
        name="project_down" if down else "project_up",
    )(half, *given, *before)


def activate_kernel(groups, *refs):
    pairs, (act, slope, _) = refs[: 2 * groups], refs[-3:]
    top = 0
    for i in range(groups):
        mine, other = pairs[2 * i], pairs[2 * i + 1]
        at = pl.ds(top, mine.shape[0])
        value = mine[...].astype(jnp.float32) + other[...].astype(jnp.float32)
        gate = 0.5 * (1.0 + lax.erf(value * SQRT_HALF))
        act[at, :] = (value * gate).astype(act.dtype)
        slope[at, :] = gate + value * jnp.exp(-0.5 * value * value) * INV_ROOT_TWO_PI
        top += mine.shape[0]


def backward_kernel(groups, *refs):
    pairs, slope, out = refs[: 2 * groups], refs[2 * groups], refs[-2]
    top = 0
    for i in range(groups):
        mine, other = pairs[2 * i], pairs[2 * i + 1]
        at = pl.ds(top, mine.shape[0])
        value = mine[...].astype(jnp.float32) + other[...].astype(jnp.float32)
        out[at, :] = (value * slope[at, :]).astype(out.dtype)
        top += mine.shape[0]


def column_spec(array, tile, offset):
    return pl.BlockSpec((array.shape[0], tile), lambda step: (0, offset // tile + step))


def pointwise(pairs, width, slope, before):
    offsets = [at for _, _, at in pairs] + ([slope[1]] if slope else [])
    tile = tile_of(width, 384, *offsets)
    count = sum(mine.shape[0] for mine, _, _ in pairs)
    given, specs = [], []
    for mine, other, at in pairs:
        given += [mine, other]
        specs += [column_spec(mine, tile, at)] * 2
    whole = pl.BlockSpec((count, tile), lambda step: (0, step))
    result = jax.ShapeDtypeStruct((count, width), jnp.bfloat16)
    if slope:
        given.append(slope[0])
        specs.append(column_spec(slope[0], tile, slope[1]))
        kernel, shapes, outs = backward_kernel, (result, TICKET), (whole, ANY)
    else:
        kernel = activate_kernel
        shapes = (result, jax.ShapeDtypeStruct((count, width), jnp.float32), TICKET)
        outs = (whole, whole, ANY)
    return pl.pallas_call(
        functools.partial(kernel, len(pairs)),
        out_shape=shapes,
        grid=(width // tile,),
        in_specs=specs + [ANY] * len(before),
        out_specs=outs,
        compiler_params=pltpu.CompilerParams(vmem_limit_bytes=10 * 1024 * 1024),
        cost_estimate=BRIEF,
        name="hidden_gradient" if slope else "activation",
    )(*given, *before)


def stack_kernel(pieces, transposed, *refs):
    outs = refs[-3:] if transposed else refs[-2:]
    top = 0
    for piece in refs[:pieces]:
        at = pl.ds(top, piece.shape[0])
        outs[0][at, :] = piece[...]
        if transposed:
            outs[1][:, at] = piece[...].T
        top += piece.shape[0]


def stack(pieces, transposed, before):
    count, model = sum(piece.shape[0] for piece in pieces), pieces[0].shape[1]
    shapes = [(count, model), (model, count)] if transposed else [(count, model)]
    return pl.pallas_call(
        functools.partial(stack_kernel, len(pieces), transposed),
        out_shape=(*(jax.ShapeDtypeStruct(shape, pieces[0].dtype) for shape in shapes), TICKET),
        in_specs=[VMEM] * len(pieces) + [ANY] * len(before),
        out_specs=(VMEM,) * len(shapes) + (ANY,),
        compiler_params=pltpu.CompilerParams(vmem_limit_bytes=12 * 1024 * 1024),
        cost_estimate=BRIEF,
        name="stack",
    )(*pieces, *before)


def begin_kernel(*refs):
    pass


def begin(scalars, arrays):
    return pl.pallas_call(
        begin_kernel,
        out_shape=TICKET,
        in_specs=[pl.BlockSpec(memory_space=pltpu.SMEM)] * len(scalars) + [ANY] * len(arrays),
        out_specs=ANY,
        compiler_params=pltpu.CompilerParams(vmem_limit_bytes=1024 * 1024),
        cost_estimate=BRIEF,
        name="begin",
    )(*scalars, *arrays)


def copy_kernel(source, *refs):
    refs[-2][...] = source[...]


def late(source, before):
    return pl.pallas_call(
        copy_kernel,
        out_shape=(jax.ShapeDtypeStruct(source.shape, source.dtype), TICKET),
        in_specs=[VMEM] + [ANY] * len(before),
        out_specs=(VMEM, ANY),
        compiler_params=pltpu.CompilerParams(vmem_limit_bytes=4 * 1024 * 1024),
        cost_estimate=BRIEF,
        name="late",
    )(source, *before)


def gradient_kernel(down, parts, span, start, half, mask, *refs):
    fixed, *moving = refs[: 1 + parts]
    out = refs[-2]
    part, step = pl.program_id(0), pl.program_id(1)
    tile = out.shape[0 if down else 1]
    first = ((half[0] ^ part) * span + start + step * tile) // BLOCK

    def store(source):
        left, right = (source, fixed) if down else (fixed, source)
        dims = (((0 if down else 1,), (0,)), ((), ()))
        value = lax.dot_general(left[...], right[...], dims, preferred_element_type=jnp.float32)
        bits = spread_mask(mask, down, first, tile)
        for i in range(bits.shape[0]):
            block = value[i * BLOCK : (i + 1) * BLOCK, :].astype(out.dtype)
            out[pl.ds(i * BLOCK, BLOCK), :] = block * bits[i : i + 1, :]

    for i, source in enumerate(moving):
        pl.when(part == i)(functools.partial(store, source))


def gradient(fixed, moving, mask, down, half, start, units, out, before):
    span = units // CORES
    count, width = moving[0].shape
    parts = len(moving)
    model = fixed.shape[1 if down else 0]
    tile = tile_of(width, 768, start)
    steps = width // tile
    shape = (units, model) if down else (model, units)

    def unit_block(part, step, half):
        return (half[0] ^ part) * (span // tile) + start // tile + step

    specs = [pl.BlockSpec(array.shape, lambda *at: (0, 0)) for array in (mask, fixed)]
    for i in range(parts):
        rest = 0 if i else steps - 1

        def place(part, step, half, i=i, rest=rest):
            return (0, jnp.where(part == i, step, rest))

        specs.append(pl.BlockSpec((count, tile), place))
    if down:
        out_spec = pl.BlockSpec((tile, model), lambda *at: (unit_block(*at), 0))
    else:
        out_spec = pl.BlockSpec((model, tile), lambda *at: (0, unit_block(*at)))
    given = [mask, fixed, *moving]
    aliases = {}
    if out is not None:
        given.append(out)
        specs.append(ANY)
        aliases = {1 + 2 + parts: 0}
    return pl.pallas_call(
        functools.partial(gradient_kernel, down, parts, span, start),
        out_shape=(jax.ShapeDtypeStruct(shape, jnp.bfloat16), TICKET),
        grid_spec=pltpu.PrefetchScalarGridSpec(
            num_scalar_prefetch=1,
            grid=(parts, steps),
            in_specs=specs + [ANY] * len(before),
            out_specs=(out_spec, ANY),
        ),
        input_output_aliases=aliases,
        compiler_params=pltpu.CompilerParams(vmem_limit_bytes=VMEM_BYTES),
        cost_estimate=BRIEF,
        name="down_gradient" if down else "up_gradient",
    )(half, *given, *before)


def on_device(n_row, n_col, tokens, cotangent, up_weight, down_weight, up_mask, down_mask):
    units = up_weight.shape[1]
    span = units // CORES
    chips = n_col // CORES
    core = lax.axis_index("col") % CORES
    mine = core.astype(jnp.int32).reshape(1)
    other = 1 - mine

    def turn(value, by):
        return lax.ppermute(value, "row", [(i, (i + by) % n_row) for i in range(n_row)])

    def core_swap(value):
        return lax.ppermute(value, "col", [(i, i ^ 1) for i in range(n_col)])

    def chip_swap(value):
        hop = 1
        while 2 * hop < chips:
            value = value + lax.ppermute(value, "col", [(i, i ^ (CORES * hop)) for i in range(n_col)])
            hop *= 2
        if chips == 1:
            return value, jnp.zeros_like(value)
        return value, lax.ppermute(value, "col", [(i, i ^ (CORES * hop)) for i in range(n_col)])

    lanes = span // BLOCK

    def cuts(eighths):
        if any(lanes * size % 8 for size in eighths):
            eighths = [*eighths[:-2], eighths[-2] + eighths[-1]]
        ends = [span * sum(eighths[: i + 1]) // 8 for i in range(len(eighths))]
        return [(end - span * size // 8, span * size // 8) for size, end in zip(eighths, ends)]

    chunks = {name: cuts(eighths) for name, eighths in CUTS.items()}
    own = tokens.shape[0]
    inputs = {"h0": (tokens, own), "g0": (cotangent, own)}
    weights = {"h": (up_weight, up_mask), "g": (down_weight, down_mask)}
    near = sorted({1, n_row - 1} - {0}) if n_row > 1 else []
    turns = [near[:1], near[1:], [by for by in range(1, n_row) if by not in near]]
    shards = {"x": tokens, "c": cotangent}
    moves, sent, sums, stored, slopes, acts, hidden, grads = {}, {}, {}, [], [], {}, {}, {}
    before = [begin([mine, other], [up_mask, down_mask])]

    def step(call, *args):
        nonlocal before
        *results, ticket = call(*args, before)
        before = [ticket]
        return results[0] if len(results) == 1 else results

    def covering(found, start, width):
        return next(one for one in found if one[0] <= start and start + width <= one[0] + one[1])

    def product(key, side, start, width, arrived):
        rows, count = inputs[key]
        half, down = (mine, other)[side], key[0] == "g"
        if key[1] == "0":
            weight, mask = weights[key[0]]
            result, kept = step(project, rows, count, weight, mask, down, half, span, start, 0, width, arrived)
            stored.append((start, width, key[0], side, kept))
            return result
        at, _, _, _, kept = covering([one for one in stored if one[2:4] == (key[0], side)], start, width)
        return step(project, rows, count, kept, None, down, half, span, start, start - at, width, arrived)

    def pairs(kind, start, width):
        found = []
        for key in (kind + "0", kind + "1") if n_row > 1 else (kind + "0",):
            at, _, value, arrived = covering(sums[key], start, width)
            found.append((value, arrived, start - at))
        return found

    def run(action, name, at):
        if action == "turn":
            if turns[at]:
                source = step(late, shards[name])
                moves[name, at] = [turn(source, by) for by in turns[at]]
            else:
                moves[name, at] = []
            return
        if action == "stack":
            pieces = [shards[name], *(piece for i in range(3) for piece in moves[name, i])]
            if name == "x":
                inputs["h1"], stacks["x"] = step(stack, pieces, True)
                inputs["h1"] = (inputs["h1"], own * (n_row - 1))
            else:
                stacks["c"] = step(stack, pieces, False)
                inputs["g1"] = (stacks["c"], own * (n_row - 1))
            return
        if name not in chunks or at >= len(chunks[name]):
            return
        if n_row == 1 and name[1:] == "1":
            return
        start, width = chunks[name][at]
        if action == "send":
            value = product(name[:2], 1, start, width, None)
            sent.setdefault(name[:2], []).append((start, width, core_swap(value)))
        elif action == "add":
            first, _, arrived = covering(sent[name], start, width)
            value, arrived = chip_swap(product(name, 0, start, width, (arrived, start - first)))
            sums.setdefault(name, []).append((start, width, value, arrived))
            moves[name, at] = [arrived]
        elif action == "act":
            act, slope = step(pointwise, pairs("h", start, width), width, None)
            slopes.append((start, width, slope))
            acts[at] = act, core_swap(act)
        elif action == "down":
            grads["down"] = step(
                gradient, stacks["c"], acts[at], down_mask, True, mine, start, units, grads.get("down")
            )
        elif action == "hidden":
            first, _, slope = covering(slopes, start, width)
            value = step(pointwise, pairs("g", start, width), width, (slope, start - first))
            hidden[at] = value, core_swap(value)
        else:
            moving = {"up": hidden[at], "upmine": hidden[at][:1], "upother": hidden[at][1:]}[action]
            half = other if action == "upother" else mine
            grads["up"] = step(gradient, stacks["x"], moving, up_mask, False, half, start, units, grads.get("up"))

    stacks = {}
    for action, name, at, *ended in ORDER:
        for transfer in ended:
            before += moves.get(transfer, [])
        run(action, name, at)
    return grads["up"], grads["down"]


def solution(mesh):
    placed = (
        P(("groups", "row"), "col"),
        P(("groups", "row"), "col"),
        P("col", "row"),
        P("row", "col"),
        P("col", "row"),
        P("row", "col"),
    )
    return jax.shard_map(
        functools.partial(on_device, mesh.shape["row"], mesh.shape["col"]),
        mesh=mesh,
        in_specs=placed,
        out_specs=(P(("groups", "col"), "row"), P(("groups", "row"), "col")),
        check_vma=False,
    )
```

```python
import functools

import jax
import jax.numpy as jnp
from jax import lax
from jax.experimental import pallas as pl
from jax.experimental.pallas import tpu as pltpu
from jax.sharding import PartitionSpec as P

BLOCK = 128
CORES = 2
VMEM_BYTES = 20 * 1024 * 1024

SQRT_HALF = 0.7071067811865476
INV_ROOT_TWO_PI = 0.3989422804014327

ANY = pl.BlockSpec(memory_space=pl.ANY)
VMEM = pl.BlockSpec(memory_space=pltpu.VMEM)

TICKET = jax.ShapeDtypeStruct((8, 128), jnp.float32)

BRIEF = pl.CostEstimate(flops=10**10, bytes_accessed=0, transcendentals=0)


CUTS = {
    "h0": (2, 2, 4),
    "h0s": (2, 2, 4),
    "g0": (4, 4),
    "g0s": (4, 4),
    "h1": (2, 2, 4),
    "h1s": (2, 2, 4),
    "g1": (2, 2, 2, 1, 1),
    "g1s": (2, 2, 2, 2),
    "a": (2, 2, 4),
    "e": (2, 2, 2, 1, 1),
}

ORDER = [
    ("send", "h0s", 0),
    ("turn", "x", 0),
    ("turn", "x", 1),
    ("send", "h0s", 1),
    ("add", "h0", 0),
    ("send", "h0s", 2),
    ("add", "h0", 1),
    ("send", "g0s", 0, ("x", 1)),
    ("turn", "x", 2),
    ("add", "h0", 2),
    ("send", "g0s", 1, ("h0", 0)),
    ("add", "g0", 0),
    ("add", "g0", 1, ("x", 0)),
    ("stack", "x", 0, ("h0", 2)),
    ("turn", "c", 0),
    ("send", "h1s", 0),
    ("send", "h1s", 2),
    ("send", "h1s", 1, ("g0", 0), ("h0", 1)),
    ("add", "h1", 0),
    ("turn", "c", 2),
    ("turn", "c", 1),
    ("add", "h1", 1),
    ("add", "h1", 2, ("g0", 1)),
    ("act", "a", 0),
    ("act", "a", 1, ("c", 0)),
    ("stack", "c", 0),
    ("send", "g1s", 0),
    ("down", "a", 0),
    ("add", "g1", 0),
    ("send", "g1s", 1),
    ("down", "a", 1),
    ("add", "g1", 1),
    ("send", "g1s", 2),
    ("send", "g1s", 3),
    ("act", "a", 2),
    ("add", "g1", 2),
    ("add", "g1", 3),
    ("add", "g1", 4),
    ("down", "a", 2),
    ("hidden", "e", 0),
    ("hidden", "e", 1),
    ("up", "e", 0),
    ("up", "e", 1),
    ("hidden", "e", 2),
    ("upmine", "e", 2),
    ("upother", "e", 2),
    ("hidden", "e", 3),
    ("upmine", "e", 3),
    ("upother", "e", 3),
    ("hidden", "e", 4),
    ("upmine", "e", 4),
    ("upother", "e", 4),
]


def tile_of(extent, most, *offsets):
    return max(
        width
        for width in range(BLOCK, most + 1, BLOCK)
        if all(size % width == 0 for size in (extent, *offsets))
    )


def spread_mask(mask, rows, columns):
    tall, wide = mask.shape
    bits = mask[...].astype(jnp.bfloat16)
    if rows[1] != tall:
        at = (rows[1], tall)
        pick = lax.broadcasted_iota(jnp.int32, at, 0) + rows[0] == lax.broadcasted_iota(jnp.int32, at, 1)
        bits = jnp.dot(pick.astype(jnp.bfloat16), bits, preferred_element_type=jnp.float32).astype(jnp.bfloat16)
    at = (wide, columns[1] * BLOCK)
    pick = lax.broadcasted_iota(jnp.int32, at, 1) // BLOCK + columns[0] == lax.broadcasted_iota(jnp.int32, at, 0)
    return jnp.dot(bits, pick.astype(jnp.bfloat16), preferred_element_type=jnp.float32).astype(jnp.bfloat16)


def units_at(down, first, width):
    run = pl.ds(first, width)
    return (run, slice(None)) if down else (slice(None), run)


def project_kernel(fresh, down, summed, waits, span, start, offset, skip, tile, half, *refs):
    refs = list(refs)
    rows = refs.pop(0)
    source = refs.pop(0)
    mask = refs.pop(0) if fresh else None
    arrived = refs.pop(0) if summed else None
    refs = refs[waits:]
    out = refs.pop(0)
    kept, sems = (refs[0], refs[-1]) if fresh else (source, None)
    steps = out.shape[1] // tile
    begin = half[0] * span + start

    def copy(step):
        here = pl.multiple_of(begin + step * tile, BLOCK)
        there = kept.at[units_at(down, pl.multiple_of(step * tile, BLOCK), tile)]
        return pltpu.make_async_copy(source.at[units_at(down, here, tile)], there, sems.at[step])

    for step in range(steps if fresh else 0):
        copy(step).start()
    inputs = rows[pl.ds(rows.shape[0] - out.shape[0], out.shape[0]), :]

    def chunk(step, carry):
        first = skip + step * tile
        if steps > 1:
            first = pl.multiple_of(first, BLOCK)
        if fresh:
            run = ((begin + step * tile) // BLOCK, tile // BLOCK)
            bits = spread_mask(mask, run, (0, mask.shape[1])) if down else spread_mask(mask, (0, mask.shape[0]), run)
            copy(step).wait()
            for i in range(bits.shape[0]):
                if down:
                    at = (pl.ds(first + i * BLOCK, BLOCK), slice(None))
                else:
                    at = (pl.ds(i * BLOCK, BLOCK), pl.ds(first, tile))
                kept[at] = kept[at] * bits[i : i + 1, :]
        total = lax.dot_general(
            inputs,
            kept[units_at(down, first, tile)],
            (((1,), (1 if down else 0,)), ((), ())),
            preferred_element_type=jnp.float32,
        )
        here = step * tile if steps == 1 else pl.multiple_of(step * tile, BLOCK)
        if summed:
            total = total + arrived[:, pl.ds(pl.multiple_of(offset + here, BLOCK), tile)].astype(jnp.float32)
        out[:, pl.ds(here, tile)] = total.astype(out.dtype)
        return carry

    if steps == 1:
        chunk(0, 0)
    else:
        lax.fori_loop(0, steps, chunk, 0)


def project(inputs, count, weight, mask, down, half, span, start, skip, width, arrived, before):
    fresh = mask is not None
    tile = tile_of(width, 768)
    if fresh:
        given = [inputs, pltpu.with_memory_space_constraint(weight, pltpu.HBM), mask]
        specs = [VMEM, ANY, VMEM]
    else:
        given = [inputs, pltpu.with_memory_space_constraint(weight, pltpu.VMEM)]
        specs = [VMEM, VMEM]
    if arrived:
        given.append(arrived[0])
        specs.append(VMEM)
    shapes = [jax.ShapeDtypeStruct((count, width), jnp.bfloat16)]
    if fresh:
        model = weight.shape[1 if down else 0]
        shapes.append(pltpu.VMEM((width, model) if down else (model, width), weight.dtype))
    offset = arrived[1] if arrived else 0
    return pl.pallas_call(
        functools.partial(
            project_kernel, fresh, down, bool(arrived), len(before), span, start, offset, skip, tile
        ),
        out_shape=(*shapes, TICKET),
        in_specs=[pl.BlockSpec(memory_space=pltpu.SMEM)] + specs + [ANY] * len(before),
        out_specs=(VMEM,) * len(shapes) + (ANY,),
        scratch_shapes=[pltpu.SemaphoreType.DMA((width // tile,))] if fresh else [],
        compiler_params=pltpu.CompilerParams(vmem_limit_bytes=12 * 1024 * 1024),
        cost_estimate=BRIEF,
        name="project_down" if down else "project_up",
    )(half, *given, *before)


def activate_kernel(groups, *refs):
    pairs, (act, slope, _) = refs[: 2 * groups], refs[-3:]
    top = 0
    for i in range(groups):
        mine, other = pairs[2 * i], pairs[2 * i + 1]
        at = pl.ds(top, mine.shape[0])
        value = mine[...].astype(jnp.float32) + other[...].astype(jnp.float32)
        gate = 0.5 * (1.0 + lax.erf(value * SQRT_HALF))
        act[at, :] = (value * gate).astype(act.dtype)
        slope[at, :] = gate + value * jnp.exp(-0.5 * value * value) * INV_ROOT_TWO_PI
        top += mine.shape[0]


def backward_kernel(groups, *refs):
    pairs, slope, out = refs[: 2 * groups], refs[2 * groups], refs[-2]
    top = 0
    for i in range(groups):
        mine, other = pairs[2 * i], pairs[2 * i + 1]
        at = pl.ds(top, mine.shape[0])
        value = mine[...].astype(jnp.float32) + other[...].astype(jnp.float32)
        out[at, :] = (value * slope[at, :]).astype(out.dtype)
        top += mine.shape[0]


def column_spec(array, tile, offset):
    return pl.BlockSpec((array.shape[0], tile), lambda step: (0, offset // tile + step))


def pointwise(pairs, width, slope, before):
    offsets = [at for _, _, at in pairs] + ([slope[1]] if slope else [])
    tile = tile_of(width, 384, *offsets)
    count = sum(mine.shape[0] for mine, _, _ in pairs)
    given, specs = [], []
    for mine, other, at in pairs:
        given += [mine, other]
        specs += [column_spec(mine, tile, at)] * 2
    whole = pl.BlockSpec((count, tile), lambda step: (0, step))
    result = jax.ShapeDtypeStruct((count, width), jnp.bfloat16)
    if slope:
        given.append(slope[0])
        specs.append(column_spec(slope[0], tile, slope[1]))
        kernel, shapes, outs = backward_kernel, (result, TICKET), (whole, ANY)
    else:
        kernel = activate_kernel
        shapes = (result, jax.ShapeDtypeStruct((count, width), jnp.float32), TICKET)
        outs = (whole, whole, ANY)
    return pl.pallas_call(
        functools.partial(kernel, len(pairs)),
        out_shape=shapes,
        grid=(width // tile,),
        in_specs=specs + [ANY] * len(before),
        out_specs=outs,
        compiler_params=pltpu.CompilerParams(vmem_limit_bytes=10 * 1024 * 1024),
        cost_estimate=BRIEF,
        name="hidden_gradient" if slope else "activation",
    )(*given, *before)


def stack_kernel(pieces, transposed, *refs):
    outs = refs[-3:] if transposed else refs[-2:]
    top = 0
    for piece in refs[:pieces]:
        at = pl.ds(top, piece.shape[0])
        outs[0][at, :] = piece[...]
        if transposed:
            outs[1][:, at] = piece[...].T
        top += piece.shape[0]


def stack(pieces, transposed, before):
    count, model = sum(piece.shape[0] for piece in pieces), pieces[0].shape[1]
    shapes = [(count, model), (model, count)] if transposed else [(count, model)]
    return pl.pallas_call(
        functools.partial(stack_kernel, len(pieces), transposed),
        out_shape=(*(jax.ShapeDtypeStruct(shape, pieces[0].dtype) for shape in shapes), TICKET),
        in_specs=[VMEM] * len(pieces) + [ANY] * len(before),
        out_specs=(VMEM,) * len(shapes) + (ANY,),
        compiler_params=pltpu.CompilerParams(vmem_limit_bytes=12 * 1024 * 1024),
        cost_estimate=BRIEF,
        name="stack",
    )(*pieces, *before)


def begin_kernel(*refs):
    pass


def begin(scalars, arrays):
    return pl.pallas_call(
        begin_kernel,
        out_shape=TICKET,
        in_specs=[pl.BlockSpec(memory_space=pltpu.SMEM)] * len(scalars) + [ANY] * len(arrays),
        out_specs=ANY,
        compiler_params=pltpu.CompilerParams(vmem_limit_bytes=1024 * 1024),
        cost_estimate=BRIEF,
        name="begin",
    )(*scalars, *arrays)


def copy_kernel(source, *refs):
    refs[-2][...] = source[...]


def late(source, before):
    return pl.pallas_call(
        copy_kernel,
        out_shape=(jax.ShapeDtypeStruct(source.shape, source.dtype), TICKET),
        in_specs=[VMEM] + [ANY] * len(before),
        out_specs=(VMEM, ANY),
        compiler_params=pltpu.CompilerParams(vmem_limit_bytes=4 * 1024 * 1024),
        cost_estimate=BRIEF,
        name="late",
    )(source, *before)


def gradient_kernel(down, parts, span, start, half, mask, *refs):
    fixed, *moving = refs[: 1 + parts]
    out = refs[-2]
    part, step = pl.program_id(0), pl.program_id(1)
    tile = out.shape[0 if down else 1]
    first = ((half[0] ^ part) * span + start + step * tile) // BLOCK

    whole = out.shape[0]
    part_rows = tile_of(whole, 768 if down else 1536)

    def unit_columns(*at):
        if parts == 1:
            return moving[0][at]
        return jnp.where(part == 0, moving[0][at], moving[1][at])

    def rows(i, carry):
        at = pl.ds(pl.multiple_of(i * part_rows, BLOCK), part_rows)
        blocks = part_rows // BLOCK
        if down:
            left, right, dims = unit_columns(slice(None), at), fixed[...], (((0,), (0,)), ((), ()))
            bits = spread_mask(mask, (first + i * blocks, blocks), (0, mask.shape[1]))
        else:
            left, right, dims = fixed[at, :], unit_columns(slice(None), slice(None)), (((1,), (0,)), ((), ()))
            bits = spread_mask(mask, (i * blocks, blocks), (first, tile // BLOCK))
        value = lax.dot_general(left, right, dims, preferred_element_type=jnp.float32)
        for j in range(blocks):
            block = value[j * BLOCK : (j + 1) * BLOCK, :].astype(out.dtype)
            here = pl.multiple_of(i * part_rows + j * BLOCK, BLOCK)
            out[pl.ds(here, BLOCK), :] = block * bits[j : j + 1, :]
        return carry

    lax.fori_loop(0, whole // part_rows, rows, 0)


def gradient(fixed, moving, mask, down, half, start, units, out, before):
    span = units // CORES
    count, width = moving[0].shape
    parts = len(moving)
    model = fixed.shape[1 if down else 0]
    tile = tile_of(width, 768, start)
    steps = width // tile
    shape = (units, model) if down else (model, units)

    def unit_block(part, step, half):
        return (half[0] ^ part) * (span // tile) + start // tile + step

    specs = [pl.BlockSpec(array.shape, lambda *at: (0, 0)) for array in (mask, fixed)]
    for i in range(parts):
        rest = 0 if i else steps - 1

        def place(part, step, half, i=i, rest=rest):
            return (0, jnp.where(part == i, step, rest))

        specs.append(pl.BlockSpec((count, tile), place))
    if down:
        out_spec = pl.BlockSpec((tile, model), lambda *at: (unit_block(*at), 0))
    else:
        out_spec = pl.BlockSpec((model, tile), lambda *at: (0, unit_block(*at)))
    given = [mask, fixed, *moving]
    aliases = {}
    if out is not None:
        given.append(out)
        specs.append(ANY)
        aliases = {1 + 2 + parts: 0}
    return pl.pallas_call(
        functools.partial(gradient_kernel, down, parts, span, start),
        out_shape=(jax.ShapeDtypeStruct(shape, jnp.bfloat16), TICKET),
        grid_spec=pltpu.PrefetchScalarGridSpec(
            num_scalar_prefetch=1,
            grid=(parts, steps),
            in_specs=specs + [ANY] * len(before),
            out_specs=(out_spec, ANY),
        ),
        input_output_aliases=aliases,
        compiler_params=pltpu.CompilerParams(vmem_limit_bytes=VMEM_BYTES),
        cost_estimate=BRIEF,
        name="down_gradient" if down else "up_gradient",
    )(half, *given, *before)


def on_device(n_row, n_col, tokens, cotangent, up_weight, down_weight, up_mask, down_mask):
    units = up_weight.shape[1]
    span = units // CORES
    chips = n_col // CORES
    core = lax.axis_index("col") % CORES
    mine = core.astype(jnp.int32).reshape(1)
    other = 1 - mine

    def turn(value, by):
        return lax.ppermute(value, "row", [(i, (i + by) % n_row) for i in range(n_row)])

    def core_swap(value):
        return lax.ppermute(value, "col", [(i, i ^ 1) for i in range(n_col)])

    def chip_swap(value):
        hop = 1
        while 2 * hop < chips:
            value = value + lax.ppermute(value, "col", [(i, i ^ (CORES * hop)) for i in range(n_col)])
            hop *= 2
        if chips == 1:
            return value, jnp.zeros_like(value)
        return value, lax.ppermute(value, "col", [(i, i ^ (CORES * hop)) for i in range(n_col)])

    lanes = span // BLOCK

    def cuts(eighths):
        if any(lanes * size % 8 for size in eighths):
            eighths = [*eighths[:-2], eighths[-2] + eighths[-1]]
        ends = [span * sum(eighths[: i + 1]) // 8 for i in range(len(eighths))]
        return [(end - span * size // 8, span * size // 8) for size, end in zip(eighths, ends)]

    chunks = {name: cuts(eighths) for name, eighths in CUTS.items()}
    own = tokens.shape[0]
    inputs = {"h0": (tokens, own), "g0": (cotangent, own)}
    weights = {"h": (up_weight, up_mask), "g": (down_weight, down_mask)}
    near = sorted({1, n_row - 1} - {0}) if n_row > 1 else []
    turns = [near[:1], near[1:], [by for by in range(1, n_row) if by not in near]]
    shards = {"x": tokens, "c": cotangent}
    moves, sent, sums, stored, slopes, acts, hidden, grads = {}, {}, {}, [], [], {}, {}, {}
    before = [begin([mine, other], [up_mask, down_mask])]

    def step(call, *args):
        nonlocal before
        *results, ticket = call(*args, before)
        before = [ticket]
        return results[0] if len(results) == 1 else results

    def covering(found, start, width):
        return next(one for one in found if one[0] <= start and start + width <= one[0] + one[1])

    def product(key, side, start, width, arrived):
        rows, count = inputs[key]
        half, down = (mine, other)[side], key[0] == "g"
        if key[1] == "0":
            weight, mask = weights[key[0]]
            result, kept = step(project, rows, count, weight, mask, down, half, span, start, 0, width, arrived)
            stored.append((start, width, key[0], side, kept))
            return result
        at, _, _, _, kept = covering([one for one in stored if one[2:4] == (key[0], side)], start, width)
        return step(project, rows, count, kept, None, down, half, span, start, start - at, width, arrived)

    def pairs(kind, start, width):
        found = []
        for key in (kind + "0", kind + "1") if n_row > 1 else (kind + "0",):
            at, _, value, arrived = covering(sums[key], start, width)
            found.append((value, arrived, start - at))
        return found

    def run(action, name, at):
        if action == "turn":
            if turns[at]:
                source = step(late, shards[name])
                moves[name, at] = [turn(source, by) for by in turns[at]]
            else:
                moves[name, at] = []
            return
        if action == "stack":
            pieces = [shards[name], *(piece for i in range(3) for piece in moves[name, i])]
            if name == "x":
                inputs["h1"], stacks["x"] = step(stack, pieces, True)
                inputs["h1"] = (inputs["h1"], own * (n_row - 1))
            else:
                stacks["c"] = step(stack, pieces, False)
                inputs["g1"] = (stacks["c"], own * (n_row - 1))
            return
        if name not in chunks or at >= len(chunks[name]):
            return
        if n_row == 1 and name[1:] == "1":
            return
        start, width = chunks[name][at]
        if action == "send":
            value = product(name[:2], 1, start, width, None)
            sent.setdefault(name[:2], []).append((start, width, core_swap(value)))
        elif action == "add":
            first, _, arrived = covering(sent[name], start, width)
            value, arrived = chip_swap(product(name, 0, start, width, (arrived, start - first)))
            sums.setdefault(name, []).append((start, width, value, arrived))
            moves[name, at] = [arrived]
        elif action == "act":
            act, slope = step(pointwise, pairs("h", start, width), width, None)
            slopes.append((start, width, slope))
            acts[at] = act, core_swap(act)
        elif action == "down":
            grads["down"] = step(
                gradient, stacks["c"], acts[at], down_mask, True, mine, start, units, grads.get("down")
            )
        elif action == "hidden":
            first, _, slope = covering(slopes, start, width)
            value = step(pointwise, pairs("g", start, width), width, (slope, start - first))
            hidden[at] = value, core_swap(value)
        else:
            moving = {"up": hidden[at], "upmine": hidden[at][:1], "upother": hidden[at][1:]}[action]
            half = other if action == "upother" else mine
            grads["up"] = step(gradient, stacks["x"], moving, up_mask, False, half, start, units, grads.get("up"))

    stacks = {}
    for action, name, at, *ended in ORDER:
        for transfer in ended:
            before += moves.get(transfer, [])
        run(action, name, at)
    return grads["up"], grads["down"]


def solution(mesh):
    placed = (
        P(("groups", "row"), "col"),
        P(("groups", "row"), "col"),
        P("col", "row"),
        P("row", "col"),
        P("col", "row"),
        P("row", "col"),
    )
    return jax.shard_map(
        functools.partial(on_device, mesh.shape["row"], mesh.shape["col"]),
        mesh=mesh,
        in_specs=placed,
        out_specs=(P(("groups", "col"), "row"), P(("groups", "row"), "col")),
        check_vma=False,
    )
```

```python
import functools

import jax
import jax.numpy as jnp
from jax import lax
from jax.experimental import pallas as pl
from jax.experimental.pallas import tpu as pltpu
from jax.sharding import PartitionSpec as P

BLOCK = 128
CORES = 2
VMEM_BYTES = 20 * 1024 * 1024

SQRT_HALF = 0.7071067811865476
INV_ROOT_TWO_PI = 0.3989422804014327

ANY = pl.BlockSpec(memory_space=pl.ANY)
VMEM = pl.BlockSpec(memory_space=pltpu.VMEM)

TICKET = jax.ShapeDtypeStruct((8, 128), jnp.float32)

BRIEF = pl.CostEstimate(flops=10**10, bytes_accessed=0, transcendentals=0)


CUTS = {
    "h0": (2, 2, 4),
    "h0s": (2, 2, 4),
    "g0": (4, 4),
    "g0s": (4, 4),
    "h1": (2, 2, 4),
    "h1s": (2, 2, 4),
    "g1": (2, 2, 2, 1, 1),
    "g1s": (2, 2, 2, 2),
    "a": (2, 2, 4),
    "e": (2, 2, 2, 1, 1),
}

ORDER = [
    ("send", "h0s", 0),
    ("turn", "x", 0),
    ("turn", "x", 1),
    ("send", "h0s", 1),
    ("add", "h0", 0),
    ("send", "h0s", 2),
    ("add", "h0", 1),
    ("send", "g0s", 0, ("x", 1)),
    ("turn", "x", 2),
    ("add", "h0", 2),
    ("send", "g0s", 1, ("h0", 0)),
    ("add", "g0", 0),
    ("add", "g0", 1, ("x", 0)),
    ("stack", "x", 0, ("h0", 2)),
    ("turn", "c", 0),
    ("send", "h1s", 0),
    ("send", "h1s", 2),
    ("send", "h1s", 1, ("g0", 0), ("h0", 1)),
    ("add", "h1", 0),
    ("turn", "c", 2),
    ("turn", "c", 1),
    ("add", "h1", 1),
    ("add", "h1", 2, ("g0", 1)),
    ("act", "a", 0),
    ("act", "a", 1, ("c", 0)),
    ("stack", "c", 0),
    ("send", "g1s", 0),
    ("down", "a", 0),
    ("add", "g1", 0),
    ("send", "g1s", 1),
    ("down", "a", 1),
    ("add", "g1", 1),
    ("send", "g1s", 2),
    ("send", "g1s", 3),
    ("act", "a", 2),
    ("add", "g1", 2),
    ("add", "g1", 3),
    ("add", "g1", 4),
    ("down", "a", 2),
    ("hidden", "e", 0),
    ("hidden", "e", 1),
    ("up", "e", 0),
    ("up", "e", 1),
    ("hidden", "e", 2),
    ("upmine", "e", 2),
    ("upother", "e", 2),
    ("hidden", "e", 3),
    ("upmine", "e", 3),
    ("upother", "e", 3),
    ("hidden", "e", 4),
    ("upmine", "e", 4),
    ("upother", "e", 4),
]


def tile_of(extent, most, *offsets):
    return max(
        width
        for width in range(BLOCK, most + 1, BLOCK)
        if all(size % width == 0 for size in (extent, *offsets))
    )


def spread_mask(mask, down, rows, columns):
    wide, tall = mask.shape if down else mask.shape[::-1]
    bits = mask[...].astype(jnp.bfloat16)
    if down or rows[1] != tall:
        at = (rows[1], tall)
        pick = lax.broadcasted_iota(jnp.int32, at, 0) + rows[0] == lax.broadcasted_iota(jnp.int32, at, 1)
        dims = (((1,), (1 if down else 0,)), ((), ()))
        bits = lax.dot_general(pick.astype(jnp.bfloat16), bits, dims, preferred_element_type=jnp.float32).astype(jnp.bfloat16)
    at = (wide, columns[1] * BLOCK)
    pick = lax.broadcasted_iota(jnp.int32, at, 1) // BLOCK + columns[0] == lax.broadcasted_iota(jnp.int32, at, 0)
    return jnp.dot(bits, pick.astype(jnp.bfloat16), preferred_element_type=jnp.float32).astype(jnp.bfloat16)


def units_at(down, first, width):
    run = pl.ds(first, width)
    return (run, slice(None)) if down else (slice(None), run)


def project_kernel(opening, fresh, down, summed, waits, span, start, offset, skip, tile, half, *refs):
    refs = list(refs)
    rows = refs.pop(0)
    source = refs.pop(0)
    mask = refs.pop(0) if fresh else None
    arrived = refs.pop(0) if summed else None
    refs = refs[waits:]
    out = refs.pop(0)
    kept = refs[0] if fresh else source
    sems = refs[2] if fresh and not opening else refs[3] if opening else None
    if opening:
        echo, held, more = refs[1], *refs[4:]
        small = [
            pltpu.make_async_copy(rows, echo, more.at[0]),
            pltpu.make_async_copy(mask, held, more.at[1]),
        ]
        for one in small:
            one.start()
        rows, mask = echo, held
    steps = out.shape[1] // tile
    begin = half[0] * span + start

    def copy(step):
        here = pl.multiple_of(begin + step * tile, BLOCK)
        there = kept.at[units_at(down, pl.multiple_of(step * tile, BLOCK), tile)]
        return pltpu.make_async_copy(source.at[units_at(down, here, tile)], there, sems.at[step])

    for step in range(steps if fresh else 0):
        copy(step).start()
    for one in small if opening else []:
        one.wait()
    inputs = rows[pl.ds(rows.shape[0] - out.shape[0], out.shape[0]), :]

    def chunk(step, carry):
        first = skip + step * tile
        if steps > 1:
            first = pl.multiple_of(first, BLOCK)
        if fresh:
            run = ((begin + step * tile) // BLOCK, tile // BLOCK)
            every = (0, mask.shape[0])
            bits = spread_mask(mask, down, run, every) if down else spread_mask(mask, down, every, run)
            copy(step).wait()
            for i in range(bits.shape[0]):
                if down:
                    at = (pl.ds(first + i * BLOCK, BLOCK), slice(None))
                else:
                    at = (pl.ds(i * BLOCK, BLOCK), pl.ds(first, tile))
                kept[at] = kept[at] * bits[i : i + 1, :]
        total = lax.dot_general(
            inputs,
            kept[units_at(down, first, tile)],
            (((1,), (1 if down else 0,)), ((), ())),
            preferred_element_type=jnp.float32,
        )
        here = step * tile if steps == 1 else pl.multiple_of(step * tile, BLOCK)
        if summed:
            total = total + arrived[:, pl.ds(pl.multiple_of(offset + here, BLOCK), tile)].astype(jnp.float32)
        out[:, pl.ds(here, tile)] = total.astype(out.dtype)
        return carry

    if steps == 1:
        chunk(0, 0)
    else:
        lax.fori_loop(0, steps, chunk, 0)


def project(inputs, count, weight, mask, down, opening, half, span, start, skip, width, arrived, before):
    fresh = mask is not None
    tile = tile_of(width, 768)
    if fresh:
        given = [inputs, pltpu.with_memory_space_constraint(weight, pltpu.HBM), mask]
        specs = [VMEM, ANY, VMEM]
        if opening:
            given = [pltpu.with_memory_space_constraint(array, pltpu.HBM) for array in (inputs, weight, mask)]
            specs = [ANY] * 3
    else:
        given = [inputs, pltpu.with_memory_space_constraint(weight, pltpu.VMEM)]
        specs = [VMEM, VMEM]
    if arrived:
        given.append(arrived[0])
        specs.append(VMEM)
    shapes = [jax.ShapeDtypeStruct((count, width), jnp.bfloat16)]
    if fresh:
        model = weight.shape[1 if down else 0]
        shapes.append(pltpu.VMEM((width, model) if down else (model, width), weight.dtype))
    scratch = [pltpu.SemaphoreType.DMA((width // tile,))] if fresh else []
    if opening:
        shapes.append(jax.ShapeDtypeStruct(inputs.shape, inputs.dtype))
        scratch += [pltpu.VMEM(mask.shape, mask.dtype), pltpu.SemaphoreType.DMA((2,))]
    offset = arrived[1] if arrived else 0
    return pl.pallas_call(
        functools.partial(
            project_kernel, opening, fresh, down, bool(arrived), len(before), span, start, offset, skip, tile
        ),
        out_shape=(*shapes, TICKET),
        in_specs=[pl.BlockSpec(memory_space=pltpu.SMEM)] + specs + [ANY] * len(before),
        out_specs=(VMEM,) * len(shapes) + (ANY,),
        scratch_shapes=scratch,
        compiler_params=pltpu.CompilerParams(vmem_limit_bytes=12 * 1024 * 1024),
        cost_estimate=BRIEF,
        name="project_down" if down else "project_up",
    )(half, *given, *before)


def activate_kernel(groups, *refs):
    pairs, (act, slope, _) = refs[: 2 * groups], refs[-3:]
    top = 0
    for i in range(groups):
        mine, other = pairs[2 * i], pairs[2 * i + 1]
        at = pl.ds(top, mine.shape[0])
        value = mine[...].astype(jnp.float32) + other[...].astype(jnp.float32)
        gate = 0.5 * (1.0 + lax.erf(value * SQRT_HALF))
        act[at, :] = (value * gate).astype(act.dtype)
        slope[at, :] = gate + value * jnp.exp(-0.5 * value * value) * INV_ROOT_TWO_PI
        top += mine.shape[0]


def backward_kernel(groups, *refs):
    pairs, slope, out = refs[: 2 * groups], refs[2 * groups], refs[-2]
    top = 0
    for i in range(groups):
        mine, other = pairs[2 * i], pairs[2 * i + 1]
        at = pl.ds(top, mine.shape[0])
        value = mine[...].astype(jnp.float32) + other[...].astype(jnp.float32)
        out[at, :] = (value * slope[at, :]).astype(out.dtype)
        top += mine.shape[0]


def column_spec(array, tile, offset):
    return pl.BlockSpec((array.shape[0], tile), lambda step: (0, offset // tile + step))


def pointwise(pairs, width, slope, before):
    offsets = [at for _, _, at in pairs] + ([slope[1]] if slope else [])
    tile = tile_of(width, 384, *offsets)
    count = sum(mine.shape[0] for mine, _, _ in pairs)
    given, specs = [], []
    for mine, other, at in pairs:
        given += [mine, other]
        specs += [column_spec(mine, tile, at)] * 2
    whole = pl.BlockSpec((count, tile), lambda step: (0, step))
    result = jax.ShapeDtypeStruct((count, width), jnp.bfloat16)
    if slope:
        given.append(slope[0])
        specs.append(column_spec(slope[0], tile, slope[1]))
        kernel, shapes, outs = backward_kernel, (result, TICKET), (whole, ANY)
    else:
        kernel = activate_kernel
        shapes = (result, jax.ShapeDtypeStruct((count, width), jnp.float32), TICKET)
        outs = (whole, whole, ANY)
    return pl.pallas_call(
        functools.partial(kernel, len(pairs)),
        out_shape=shapes,
        grid=(width // tile,),
        in_specs=specs + [ANY] * len(before),
        out_specs=outs,
        compiler_params=pltpu.CompilerParams(vmem_limit_bytes=10 * 1024 * 1024),
        cost_estimate=BRIEF,
        name="hidden_gradient" if slope else "activation",
    )(*given, *before)


def stack_kernel(pieces, transposed, *refs):
    outs = refs[-3:] if transposed else refs[-2:]
    top = 0
    for piece in refs[:pieces]:
        at = pl.ds(top, piece.shape[0])
        outs[0][at, :] = piece[...]
        if transposed:
            outs[1][:, at] = piece[...].T
        top += piece.shape[0]


def stack(pieces, transposed, before):
    count, model = sum(piece.shape[0] for piece in pieces), pieces[0].shape[1]
    shapes = [(count, model), (model, count)] if transposed else [(count, model)]
    return pl.pallas_call(
        functools.partial(stack_kernel, len(pieces), transposed),
        out_shape=(*(jax.ShapeDtypeStruct(shape, pieces[0].dtype) for shape in shapes), TICKET),
        in_specs=[VMEM] * len(pieces) + [ANY] * len(before),
        out_specs=(VMEM,) * len(shapes) + (ANY,),
        compiler_params=pltpu.CompilerParams(vmem_limit_bytes=12 * 1024 * 1024),
        cost_estimate=BRIEF,
        name="stack",
    )(*pieces, *before)


def begin_kernel(*refs):
    pass


def begin(scalars, arrays):
    return pl.pallas_call(
        begin_kernel,
        out_shape=TICKET,
        in_specs=[pl.BlockSpec(memory_space=pltpu.SMEM)] * len(scalars) + [ANY] * len(arrays),
        out_specs=ANY,
        compiler_params=pltpu.CompilerParams(vmem_limit_bytes=1024 * 1024),
        cost_estimate=BRIEF,
        name="begin",
    )(*scalars, *arrays)


def copy_kernel(source, *refs):
    refs[-2][...] = source[...]


def late(source, before):
    return pl.pallas_call(
        copy_kernel,
        out_shape=(jax.ShapeDtypeStruct(source.shape, source.dtype), TICKET),
        in_specs=[VMEM] + [ANY] * len(before),
        out_specs=(VMEM, ANY),
        compiler_params=pltpu.CompilerParams(vmem_limit_bytes=4 * 1024 * 1024),
        cost_estimate=BRIEF,
        name="late",
    )(source, *before)


def gradient_kernel(down, parts, span, start, half, mask, *refs):
    fixed, *moving = refs[: 1 + parts]
    out = refs[-2]
    part, step = pl.program_id(0), pl.program_id(1)
    tile = out.shape[0 if down else 1]
    first = ((half[0] ^ part) * span + start + step * tile) // BLOCK

    whole = out.shape[0]
    part_rows = tile_of(whole, 768 if down else 1536)

    def unit_columns(*at):
        if parts == 1:
            return moving[0][at]
        return jnp.where(part == 0, moving[0][at], moving[1][at])

    def rows(i, carry):
        at = pl.ds(pl.multiple_of(i * part_rows, BLOCK), part_rows)
        blocks = part_rows // BLOCK
        if down:
            left, right, dims = unit_columns(slice(None), at), fixed[...], (((0,), (0,)), ((), ()))
            bits = spread_mask(mask, down, (first + i * blocks, blocks), (0, mask.shape[0]))
        else:
            left, right, dims = fixed[at, :], unit_columns(slice(None), slice(None)), (((1,), (0,)), ((), ()))
            bits = spread_mask(mask, down, (i * blocks, blocks), (first, tile // BLOCK))
        value = lax.dot_general(left, right, dims, preferred_element_type=jnp.float32)
        for j in range(blocks):
            block = value[j * BLOCK : (j + 1) * BLOCK, :].astype(out.dtype)
            here = pl.multiple_of(i * part_rows + j * BLOCK, BLOCK)
            out[pl.ds(here, BLOCK), :] = block * bits[j : j + 1, :]
        return carry

    lax.fori_loop(0, whole // part_rows, rows, 0)


def gradient(fixed, moving, mask, down, half, start, units, out, before):
    span = units // CORES
    count, width = moving[0].shape
    parts = len(moving)
    model = fixed.shape[1 if down else 0]
    tile = tile_of(width, 768, start)
    steps = width // tile
    shape = (units, model) if down else (model, units)

    def unit_block(part, step, half):
        return (half[0] ^ part) * (span // tile) + start // tile + step

    specs = [pl.BlockSpec(array.shape, lambda *at: (0, 0)) for array in (mask, fixed)]
    for i in range(parts):
        rest = 0 if i else steps - 1

        def place(part, step, half, i=i, rest=rest):
            return (0, jnp.where(part == i, step, rest))

        specs.append(pl.BlockSpec((count, tile), place))
    if down:
        out_spec = pl.BlockSpec((tile, model), lambda *at: (unit_block(*at), 0))
    else:
        out_spec = pl.BlockSpec((model, tile), lambda *at: (0, unit_block(*at)))
    given = [mask, fixed, *moving]
    aliases = {}
    if out is not None:
        given.append(out)
        specs.append(ANY)
        aliases = {1 + 2 + parts: 0}
    return pl.pallas_call(
        functools.partial(gradient_kernel, down, parts, span, start),
        out_shape=(jax.ShapeDtypeStruct(shape, jnp.bfloat16), TICKET),
        grid_spec=pltpu.PrefetchScalarGridSpec(
            num_scalar_prefetch=1,
            grid=(parts, steps),
            in_specs=specs + [ANY] * len(before),
            out_specs=(out_spec, ANY),
        ),
        input_output_aliases=aliases,
        compiler_params=pltpu.CompilerParams(vmem_limit_bytes=VMEM_BYTES),
        cost_estimate=BRIEF,
        name="down_gradient" if down else "up_gradient",
    )(half, *given, *before)


def on_device(n_row, n_col, tokens, cotangent, up_weight, down_weight, up_mask, down_mask):
    units = up_weight.shape[1]
    span = units // CORES
    chips = n_col // CORES
    core = lax.axis_index("col") % CORES
    mine = core.astype(jnp.int32).reshape(1)
    other = 1 - mine

    def turn(value, by):
        return lax.ppermute(value, "row", [(i, (i + by) % n_row) for i in range(n_row)])

    def core_swap(value):
        return lax.ppermute(value, "col", [(i, i ^ 1) for i in range(n_col)])

    def chip_swap(value):
        hop = 1
        while 2 * hop < chips:
            value = value + lax.ppermute(value, "col", [(i, i ^ (CORES * hop)) for i in range(n_col)])
            hop *= 2
        if chips == 1:
            return value, jnp.zeros_like(value)
        return value, lax.ppermute(value, "col", [(i, i ^ (CORES * hop)) for i in range(n_col)])

    lanes = span // BLOCK

    def cuts(eighths):
        if any(lanes * size % 8 for size in eighths):
            eighths = [*eighths[:-2], eighths[-2] + eighths[-1]]
        ends = [span * sum(eighths[: i + 1]) // 8 for i in range(len(eighths))]
        return [(end - span * size // 8, span * size // 8) for size, end in zip(eighths, ends)]

    chunks = {name: cuts(eighths) for name, eighths in CUTS.items()}
    own = tokens.shape[0]
    inputs = {"h0": (tokens, own), "g0": (cotangent, own)}
    weights = {"h": (up_weight, up_mask), "g": (down_weight, down_mask.T)}
    near = sorted({1, n_row - 1} - {0}) if n_row > 1 else []
    turns = [near[:1], near[1:], [by for by in range(1, n_row) if by not in near]]
    shards = {"x": tokens, "c": cotangent}
    moves, sent, sums, stored, slopes, acts, hidden, grads = {}, {}, {}, [], [], {}, {}, {}
    before = [begin([mine, other], [])]

    def step(call, *args):
        nonlocal before
        *results, ticket = call(*args, before)
        before = [ticket]
        return results[0] if len(results) == 1 else results

    def covering(found, start, width):
        return next(one for one in found if one[0] <= start and start + width <= one[0] + one[1])

    def product(key, side, start, width, arrived):
        rows, count = inputs[key]
        half, down = (mine, other)[side], key[0] == "g"
        if key[1] == "0":
            weight, mask = weights[key[0]]
            opening = not stored and key == "h0"
            result, kept, *echo = step(project, rows, count, weight, mask, down, opening, half, span, start, 0, width, arrived)
            if opening:
                shards["echo"] = echo[0]
            stored.append((start, width, key[0], side, kept))
            return result
        at, _, _, _, kept = covering([one for one in stored if one[2:4] == (key[0], side)], start, width)
        return step(project, rows, count, kept, None, down, False, half, span, start, start - at, width, arrived)

    def pairs(kind, start, width):
        found = []
        for key in (kind + "0", kind + "1") if n_row > 1 else (kind + "0",):
            at, _, value, arrived = covering(sums[key], start, width)
            found.append((value, arrived, start - at))
        return found

    def run(action, name, at):
        if action == "turn":
            if turns[at]:
                source = shards["echo"] if name == "x" and at < 2 else step(late, shards[name])
                moves[name, at] = [turn(source, by) for by in turns[at]]
            else:
                moves[name, at] = []
            return
        if action == "stack":
            pieces = [shards[name], *(piece for i in range(3) for piece in moves[name, i])]
            if name == "x":
                inputs["h1"], stacks["x"] = step(stack, pieces, True)
                inputs["h1"] = (inputs["h1"], own * (n_row - 1))
            else:
                stacks["c"] = step(stack, pieces, False)
                inputs["g1"] = (stacks["c"], own * (n_row - 1))
            return
        if name not in chunks or at >= len(chunks[name]):
            return
        if n_row == 1 and name[1:] == "1":
            return
        start, width = chunks[name][at]
        if action == "send":
            value = product(name[:2], 1, start, width, None)
            sent.setdefault(name[:2], []).append((start, width, core_swap(value)))
        elif action == "add":
            first, _, arrived = covering(sent[name], start, width)
            value, arrived = chip_swap(product(name, 0, start, width, (arrived, start - first)))
            sums.setdefault(name, []).append((start, width, value, arrived))
            moves[name, at] = [arrived]
        elif action == "act":
            act, slope = step(pointwise, pairs("h", start, width), width, None)
            slopes.append((start, width, slope))
            acts[at] = act, core_swap(act)
        elif action == "down":
            grads["down"] = step(
                gradient, stacks["c"], acts[at], down_mask.T, True, mine, start, units, grads.get("down")
            )
        elif action == "hidden":
            first, _, slope = covering(slopes, start, width)
            value = step(pointwise, pairs("g", start, width), width, (slope, start - first))
            hidden[at] = value, core_swap(value)
        else:
            moving = {"up": hidden[at], "upmine": hidden[at][:1], "upother": hidden[at][1:]}[action]
            half = other if action == "upother" else mine
            grads["up"] = step(gradient, stacks["x"], moving, up_mask, False, half, start, units, grads.get("up"))

    stacks = {}
    for action, name, at, *ended in ORDER:
        for transfer in ended:
            before += moves.get(transfer, [])
        run(action, name, at)
    return grads["up"], grads["down"]


def solution(mesh):
    placed = (
        P(("groups", "row"), "col"),
        P(("groups", "row"), "col"),
        P("col", "row"),
        P("row", "col"),
        P("col", "row"),
        P("row", "col"),
    )
    return jax.shard_map(
        functools.partial(on_device, mesh.shape["row"], mesh.shape["col"]),
        mesh=mesh,
        in_specs=placed,
        out_specs=(P(("groups", "col"), "row"), P(("groups", "row"), "col")),
        check_vma=False,
    )
```

```python
import functools

import jax
import jax.numpy as jnp
from jax import lax
from jax.experimental import pallas as pl
from jax.experimental.pallas import tpu as pltpu
from jax.sharding import PartitionSpec as P

BLOCK = 128
CORES = 2
VMEM_BYTES = 20 * 1024 * 1024

SQRT_HALF = 0.7071067811865476
INV_ROOT_TWO_PI = 0.3989422804014327

ANY = pl.BlockSpec(memory_space=pl.ANY)
VMEM = pl.BlockSpec(memory_space=pltpu.VMEM)

TICKET = jax.ShapeDtypeStruct((8, 128), jnp.float32)

BRIEF = pl.CostEstimate(flops=10**10, bytes_accessed=0, transcendentals=0)


CUTS = {
    "h0": (2, 2, 4),
    "h0s": (4, 4),
    "g0": (4, 4),
    "g0s": (4, 4),
    "h1": (2, 2, 4),
    "h1s": (2, 2, 4),
    "g1": (2, 2, 2, 1, 1),
    "g1s": (2, 2, 2, 2),
    "a": (2, 2, 4),
    "e": (2, 2, 2, 1, 1),
}

ORDER = [
    ("send", "h0s", 0),
    ("turn", "x", 0),
    ("send", "h0s", 1),
    ("add", "h0", 0),
    ("send", "h0s", 2),
    ("turn", "x", 1),
    ("add", "h0", 1),
    ("send", "g0s", 0),
    ("turn", "x", 2),
    ("add", "h0", 2),
    ("send", "g0s", 1, ("h0", 0)),
    ("add", "g0", 0),
    ("add", "g0", 1, ("x", 0)),
    ("turn", "c", 0, ("h0", 2)),
    ("stack", "x", 0),
    ("send", "h1s", 0),
    ("send", "h1s", 2),
    ("send", "h1s", 1, ("g0", 0), ("h0", 1)),
    ("add", "h1", 0),
    ("add", "h1", 1),
    ("turn", "c", 1),
    ("add", "h1", 2, ("g0", 1)),
    ("turn", "c", 2),
    ("act", "a", 0),
    ("act", "a", 1, ("c", 0)),
    ("stack", "c", 0),
    ("send", "g1s", 0),
    ("down", "a", 0),
    ("add", "g1", 0),
    ("send", "g1s", 1),
    ("down", "a", 1),
    ("add", "g1", 1),
    ("send", "g1s", 2),
    ("send", "g1s", 3),
    ("act", "a", 2),
    ("add", "g1", 2),
    ("add", "g1", 3),
    ("add", "g1", 4),
    ("down", "a", 2),
    ("hidden", "e", 0),
    ("hidden", "e", 1),
    ("up", "e", 0),
    ("up", "e", 1),
    ("hidden", "e", 2),
    ("upmine", "e", 2),
    ("upother", "e", 2),
    ("hidden", "e", 3),
    ("upmine", "e", 3),
    ("upother", "e", 3),
    ("hidden", "e", 4),
    ("upmine", "e", 4),
    ("upother", "e", 4),
]


def tile_of(extent, most, *offsets):
    return max(
        width
        for width in range(BLOCK, most + 1, BLOCK)
        if all(size % width == 0 for size in (extent, *offsets))
    )


def spread_mask(mask, down, rows, columns):
    wide, tall = mask.shape if down else mask.shape[::-1]
    bits = mask[...].astype(jnp.bfloat16)
    if down or rows[1] != tall:
        at = (rows[1], tall)
        pick = lax.broadcasted_iota(jnp.int32, at, 0) + rows[0] == lax.broadcasted_iota(jnp.int32, at, 1)
        dims = (((1,), (1 if down else 0,)), ((), ()))
        bits = lax.dot_general(pick.astype(jnp.bfloat16), bits, dims, preferred_element_type=jnp.float32).astype(jnp.bfloat16)
    at = (wide, columns[1] * BLOCK)
    pick = lax.broadcasted_iota(jnp.int32, at, 1) // BLOCK + columns[0] == lax.broadcasted_iota(jnp.int32, at, 0)
    return jnp.dot(bits, pick.astype(jnp.bfloat16), preferred_element_type=jnp.float32).astype(jnp.bfloat16)


def units_at(down, first, width):
    run = pl.ds(first, width)
    return (run, slice(None)) if down else (slice(None), run)


def project_kernel(opening, fresh, down, summed, waits, span, start, offset, skip, tile, half, *refs):
    refs = list(refs)
    rows = refs.pop(0)
    source = refs.pop(0)
    mask = refs.pop(0) if fresh else None
    arrived = refs.pop(0) if summed else None
    refs = refs[waits:]
    out = refs.pop(0)
    kept = refs[0] if fresh else source
    sems = refs[2] if fresh and not opening else refs[3] if opening else None
    if opening:
        echo, held, more = refs[1], *refs[4:]
        small = [
            pltpu.make_async_copy(rows, echo, more.at[0]),
            pltpu.make_async_copy(mask, held, more.at[1]),
        ]
        for one in small:
            one.start()
        rows, mask = echo, held
    steps = out.shape[1] // tile
    begin = half[0] * span + start

    def copy(step):
        here = pl.multiple_of(begin + step * tile, BLOCK)
        there = kept.at[units_at(down, pl.multiple_of(step * tile, BLOCK), tile)]
        return pltpu.make_async_copy(source.at[units_at(down, here, tile)], there, sems.at[step])

    for step in range(steps if fresh else 0):
        copy(step).start()
    for one in small if opening else []:
        one.wait()
    inputs = rows[pl.ds(rows.shape[0] - out.shape[0], out.shape[0]), :]

    def chunk(step, carry):
        first = skip + step * tile
        if steps > 1:
            first = pl.multiple_of(first, BLOCK)
        if fresh:
            run = ((begin + step * tile) // BLOCK, tile // BLOCK)
            every = (0, mask.shape[0])
            bits = spread_mask(mask, down, run, every) if down else spread_mask(mask, down, every, run)
            copy(step).wait()
            for i in range(bits.shape[0]):
                if down:
                    at = (pl.ds(first + i * BLOCK, BLOCK), slice(None))
                else:
                    at = (pl.ds(i * BLOCK, BLOCK), pl.ds(first, tile))
                kept[at] = kept[at] * bits[i : i + 1, :]
        total = lax.dot_general(
            inputs,
            kept[units_at(down, first, tile)],
            (((1,), (1 if down else 0,)), ((), ())),
            preferred_element_type=jnp.float32,
        )
        here = step * tile if steps == 1 else pl.multiple_of(step * tile, BLOCK)
        if summed:
            total = total + arrived[:, pl.ds(pl.multiple_of(offset + here, BLOCK), tile)].astype(jnp.float32)
        out[:, pl.ds(here, tile)] = total.astype(out.dtype)
        return carry

    if steps == 1:
        chunk(0, 0)
    else:
        lax.fori_loop(0, steps, chunk, 0)


def project(inputs, count, weight, mask, down, opening, half, span, start, skip, width, arrived, before):
    fresh = mask is not None
    tile = tile_of(width, 768)
    if fresh:
        given = [inputs, pltpu.with_memory_space_constraint(weight, pltpu.HBM), mask]
        specs = [VMEM, ANY, VMEM]
        if opening:
            given = [pltpu.with_memory_space_constraint(array, pltpu.HBM) for array in (inputs, weight, mask)]
            specs = [ANY] * 3
    else:
        given = [inputs, pltpu.with_memory_space_constraint(weight, pltpu.VMEM)]
        specs = [VMEM, VMEM]
    if arrived:
        given.append(arrived[0])
        specs.append(VMEM)
    shapes = [jax.ShapeDtypeStruct((count, width), jnp.bfloat16)]
    if fresh:
        model = weight.shape[1 if down else 0]
        shapes.append(pltpu.VMEM((width, model) if down else (model, width), weight.dtype))
    scratch = [pltpu.SemaphoreType.DMA((width // tile,))] if fresh else []
    if opening:
        shapes.append(jax.ShapeDtypeStruct(inputs.shape, inputs.dtype))
        scratch += [pltpu.VMEM(mask.shape, mask.dtype), pltpu.SemaphoreType.DMA((2,))]
    offset = arrived[1] if arrived else 0
    return pl.pallas_call(
        functools.partial(
            project_kernel, opening, fresh, down, bool(arrived), len(before), span, start, offset, skip, tile
        ),
        out_shape=(*shapes, TICKET),
        in_specs=[pl.BlockSpec(memory_space=pltpu.SMEM)] + specs + [ANY] * len(before),
        out_specs=(VMEM,) * len(shapes) + (ANY,),
        scratch_shapes=scratch,
        compiler_params=pltpu.CompilerParams(vmem_limit_bytes=12 * 1024 * 1024),
        cost_estimate=BRIEF,
        name="project_down" if down else "project_up",
    )(half, *given, *before)


def activate_kernel(groups, *refs):
    pairs, (act, slope, _) = refs[: 2 * groups], refs[-3:]
    top = 0
    for i in range(groups):
        mine, other = pairs[2 * i], pairs[2 * i + 1]
        at = pl.ds(top, mine.shape[0])
        value = mine[...].astype(jnp.float32) + other[...].astype(jnp.float32)
        gate = 0.5 * (1.0 + lax.erf(value * SQRT_HALF))
        act[at, :] = (value * gate).astype(act.dtype)
        slope[at, :] = gate + value * jnp.exp(-0.5 * value * value) * INV_ROOT_TWO_PI
        top += mine.shape[0]


def backward_kernel(groups, *refs):
    pairs, slope, out = refs[: 2 * groups], refs[2 * groups], refs[-2]
    top = 0
    for i in range(groups):
        mine, other = pairs[2 * i], pairs[2 * i + 1]
        at = pl.ds(top, mine.shape[0])
        value = mine[...].astype(jnp.float32) + other[...].astype(jnp.float32)
        out[at, :] = (value * slope[at, :]).astype(out.dtype)
        top += mine.shape[0]


def column_spec(array, tile, offset):
    return pl.BlockSpec((array.shape[0], tile), lambda step: (0, offset // tile + step))


def pointwise(pairs, width, slope, before):
    offsets = [at for _, _, at in pairs] + ([slope[1]] if slope else [])
    tile = tile_of(width, 384, *offsets)
    count = sum(mine.shape[0] for mine, _, _ in pairs)
    given, specs = [], []
    for mine, other, at in pairs:
        given += [mine, other]
        specs += [column_spec(mine, tile, at)] * 2
    whole = pl.BlockSpec((count, tile), lambda step: (0, step))
    result = jax.ShapeDtypeStruct((count, width), jnp.bfloat16)
    if slope:
        given.append(slope[0])
        specs.append(column_spec(slope[0], tile, slope[1]))
        kernel, shapes, outs = backward_kernel, (result, TICKET), (whole, ANY)
    else:
        kernel = activate_kernel
        shapes = (result, jax.ShapeDtypeStruct((count, width), jnp.float32), TICKET)
        outs = (whole, whole, ANY)
    return pl.pallas_call(
        functools.partial(kernel, len(pairs)),
        out_shape=shapes,
        grid=(width // tile,),
        in_specs=specs + [ANY] * len(before),
        out_specs=outs,
        compiler_params=pltpu.CompilerParams(vmem_limit_bytes=10 * 1024 * 1024),
        cost_estimate=BRIEF,
        name="hidden_gradient" if slope else "activation",
    )(*given, *before)


def stack_kernel(pieces, transposed, *refs):
    outs = refs[-3:] if transposed else refs[-2:]
    top = 0
    for piece in refs[:pieces]:
        at = pl.ds(top, piece.shape[0])
        outs[0][at, :] = piece[...]
        if transposed:
            outs[1][:, at] = piece[...].T
        top += piece.shape[0]


def stack(pieces, transposed, before):
    count, model = sum(piece.shape[0] for piece in pieces), pieces[0].shape[1]
    shapes = [(count, model), (model, count)] if transposed else [(count, model)]
    return pl.pallas_call(
        functools.partial(stack_kernel, len(pieces), transposed),
        out_shape=(*(jax.ShapeDtypeStruct(shape, pieces[0].dtype) for shape in shapes), TICKET),
        in_specs=[VMEM] * len(pieces) + [ANY] * len(before),
        out_specs=(VMEM,) * len(shapes) + (ANY,),
        compiler_params=pltpu.CompilerParams(vmem_limit_bytes=12 * 1024 * 1024),
        cost_estimate=BRIEF,
        name="stack",
    )(*pieces, *before)


def begin_kernel(*refs):
    pass


def begin(scalars, arrays):
    return pl.pallas_call(
        begin_kernel,
        out_shape=TICKET,
        in_specs=[pl.BlockSpec(memory_space=pltpu.SMEM)] * len(scalars) + [ANY] * len(arrays),
        out_specs=ANY,
        compiler_params=pltpu.CompilerParams(vmem_limit_bytes=1024 * 1024),
        cost_estimate=BRIEF,
        name="begin",
    )(*scalars, *arrays)


def copy_kernel(source, *refs):
    refs[-2][...] = source[...]


def late(source, before):
    return pl.pallas_call(
        copy_kernel,
        out_shape=(jax.ShapeDtypeStruct(source.shape, source.dtype), TICKET),
        in_specs=[VMEM] + [ANY] * len(before),
        out_specs=(VMEM, ANY),
        compiler_params=pltpu.CompilerParams(vmem_limit_bytes=4 * 1024 * 1024),
        cost_estimate=BRIEF,
        name="late",
    )(source, *before)


def gradient_kernel(down, parts, span, start, half, mask, *refs):
    fixed, *moving = refs[: 1 + parts]
    out = refs[-2]
    part, step = pl.program_id(0), pl.program_id(1)
    tile = out.shape[0 if down else 1]
    first = ((half[0] ^ part) * span + start + step * tile) // BLOCK

    whole = out.shape[0]
    part_rows = tile_of(whole, 768 if down else 1536)

    def unit_columns(*at):
        if parts == 1:
            return moving[0][at]
        return jnp.where(part == 0, moving[0][at], moving[1][at])

    def rows(i, carry):
        at = pl.ds(pl.multiple_of(i * part_rows, BLOCK), part_rows)
        blocks = part_rows // BLOCK
        if down:
            left, right, dims = unit_columns(slice(None), at), fixed[...], (((0,), (0,)), ((), ()))
            bits = spread_mask(mask, down, (first + i * blocks, blocks), (0, mask.shape[0]))
        else:
            left, right, dims = fixed[at, :], unit_columns(slice(None), slice(None)), (((1,), (0,)), ((), ()))
            bits = spread_mask(mask, down, (i * blocks, blocks), (first, tile // BLOCK))
        value = lax.dot_general(left, right, dims, preferred_element_type=jnp.float32)
        for j in range(blocks):
            block = value[j * BLOCK : (j + 1) * BLOCK, :].astype(out.dtype)
            here = pl.multiple_of(i * part_rows + j * BLOCK, BLOCK)
            out[pl.ds(here, BLOCK), :] = block * bits[j : j + 1, :]
        return carry

    lax.fori_loop(0, whole // part_rows, rows, 0)


def gradient(fixed, moving, mask, down, half, start, units, out, before):
    span = units // CORES
    count, width = moving[0].shape
    parts = len(moving)
    model = fixed.shape[1 if down else 0]
    tile = tile_of(width, 768, start)
    steps = width // tile
    shape = (units, model) if down else (model, units)

    def unit_block(part, step, half):
        return (half[0] ^ part) * (span // tile) + start // tile + step

    specs = [pl.BlockSpec(array.shape, lambda *at: (0, 0)) for array in (mask, fixed)]
    for i in range(parts):
        rest = 0 if i else steps - 1

        def place(part, step, half, i=i, rest=rest):
            return (0, jnp.where(part == i, step, rest))

        specs.append(pl.BlockSpec((count, tile), place))
    if down:
        out_spec = pl.BlockSpec((tile, model), lambda *at: (unit_block(*at), 0))
    else:
        out_spec = pl.BlockSpec((model, tile), lambda *at: (0, unit_block(*at)))
    given = [mask, fixed, *moving]
    aliases = {}
    if out is not None:
        given.append(out)
        specs.append(ANY)
        aliases = {1 + 2 + parts: 0}
    return pl.pallas_call(
        functools.partial(gradient_kernel, down, parts, span, start),
        out_shape=(jax.ShapeDtypeStruct(shape, jnp.bfloat16), TICKET),
        grid_spec=pltpu.PrefetchScalarGridSpec(
            num_scalar_prefetch=1,
            grid=(parts, steps),
            in_specs=specs + [ANY] * len(before),
            out_specs=(out_spec, ANY),
        ),
        input_output_aliases=aliases,
        compiler_params=pltpu.CompilerParams(vmem_limit_bytes=VMEM_BYTES),
        cost_estimate=BRIEF,
        name="down_gradient" if down else "up_gradient",
    )(half, *given, *before)


def on_device(n_row, n_col, tokens, cotangent, up_weight, down_weight, up_mask, down_mask):
    units = up_weight.shape[1]
    span = units // CORES
    chips = n_col // CORES
    core = lax.axis_index("col") % CORES
    mine = core.astype(jnp.int32).reshape(1)
    other = 1 - mine

    def turn(value, by):
        return lax.ppermute(value, "row", [(i, (i + by) % n_row) for i in range(n_row)])

    def core_swap(value):
        return lax.ppermute(value, "col", [(i, i ^ 1) for i in range(n_col)])

    def chip_swap(value):
        hop = 1
        while 2 * hop < chips:
            value = value + lax.ppermute(value, "col", [(i, i ^ (CORES * hop)) for i in range(n_col)])
            hop *= 2
        if chips == 1:
            return value, jnp.zeros_like(value)
        return value, lax.ppermute(value, "col", [(i, i ^ (CORES * hop)) for i in range(n_col)])

    lanes = span // BLOCK

    def cuts(eighths):
        if any(lanes * size % 8 for size in eighths):
            eighths = [*eighths[:-2], eighths[-2] + eighths[-1]]
        ends = [span * sum(eighths[: i + 1]) // 8 for i in range(len(eighths))]
        return [(end - span * size // 8, span * size // 8) for size, end in zip(eighths, ends)]

    chunks = {name: cuts(eighths) for name, eighths in CUTS.items()}
    own = tokens.shape[0]
    inputs = {"h0": (tokens, own), "g0": (cotangent, own)}
    weights = {"h": (up_weight, up_mask), "g": (down_weight, down_mask.T)}
    near = sorted({1, n_row - 1} - {0}) if n_row > 1 else []
    turns = [near[:1], near[1:], [by for by in range(1, n_row) if by not in near]]
    shards = {"x": tokens, "c": cotangent}
    moves, sent, sums, stored, slopes, acts, hidden, grads = {}, {}, {}, [], [], {}, {}, {}
    before = [begin([mine, other], [])]

    def step(call, *args):
        nonlocal before
        *results, ticket = call(*args, before)
        before = [ticket]
        return results[0] if len(results) == 1 else results

    def covering(found, start, width):
        return next(one for one in found if one[0] <= start and start + width <= one[0] + one[1])

    def product(key, side, start, width, arrived):
        rows, count = inputs[key]
        half, down = (mine, other)[side], key[0] == "g"
        if key[1] == "0":
            weight, mask = weights[key[0]]
            opening = not stored and key == "h0"
            result, kept, *echo = step(project, rows, count, weight, mask, down, opening, half, span, start, 0, width, arrived)
            if opening:
                shards["echo"] = echo[0]
            stored.append((start, width, key[0], side, kept))
            return result
        at, _, _, _, kept = covering([one for one in stored if one[2:4] == (key[0], side)], start, width)
        return step(project, rows, count, kept, None, down, False, half, span, start, start - at, width, arrived)

    def pairs(kind, start, width):
        found = []
        for key in (kind + "0", kind + "1") if n_row > 1 else (kind + "0",):
            at, _, value, arrived = covering(sums[key], start, width)
            found.append((value, arrived, start - at))
        return found

    def run(action, name, at):
        if action == "turn":
            moves[name, at] = []
            if turns[at] and at < 2:
                source = shards["echo"] if name == "x" else step(late, shards[name])
                moves[name, at] = [turn(source, by) for by in turns[at]]
            elif turns[at]:
                source = step(late, moves[name, 0][0])
                for _ in turns[at]:
                    source = turn(source, 1)
                    moves[name, at].append(source)
            return
        if action == "stack":
            pieces = [shards[name], *(piece for i in range(3) for piece in moves[name, i])]
            if name == "x":
                inputs["h1"], stacks["x"] = step(stack, pieces, True)
                inputs["h1"] = (inputs["h1"], own * (n_row - 1))
            else:
                stacks["c"] = step(stack, pieces, False)
                inputs["g1"] = (stacks["c"], own * (n_row - 1))
            return
        if name not in chunks or at >= len(chunks[name]):
            return
        if n_row == 1 and name[1:] == "1":
            return
        start, width = chunks[name][at]
        if action == "send":
            value = product(name[:2], 1, start, width, None)
            sent.setdefault(name[:2], []).append((start, width, core_swap(value)))
        elif action == "add":
            first, _, arrived = covering(sent[name], start, width)
            value, arrived = chip_swap(product(name, 0, start, width, (arrived, start - first)))
            sums.setdefault(name, []).append((start, width, value, arrived))
            moves[name, at] = [arrived]
        elif action == "act":
            act, slope = step(pointwise, pairs("h", start, width), width, None)
            slopes.append((start, width, slope))
            acts[at] = act, core_swap(act)
        elif action == "down":
            grads["down"] = step(
                gradient, stacks["c"], acts[at], down_mask.T, True, mine, start, units, grads.get("down")
            )
        elif action == "hidden":
            first, _, slope = covering(slopes, start, width)
            value = step(pointwise, pairs("g", start, width), width, (slope, start - first))
            hidden[at] = value, core_swap(value)
        else:
            moving = {"up": hidden[at], "upmine": hidden[at][:1], "upother": hidden[at][1:]}[action]
            half = other if action == "upother" else mine
            grads["up"] = step(gradient, stacks["x"], moving, up_mask, False, half, start, units, grads.get("up"))

    stacks = {}
    for action, name, at, *ended in ORDER:
        for transfer in ended:
            before += moves.get(transfer, [])
        run(action, name, at)
    return grads["up"], grads["down"]


def solution(mesh):
    placed = (
        P(("groups", "row"), "col"),
        P(("groups", "row"), "col"),
        P("col", "row"),
        P("row", "col"),
        P("col", "row"),
        P("row", "col"),
    )
    return jax.shard_map(
        functools.partial(on_device, mesh.shape["row"], mesh.shape["col"]),
        mesh=mesh,
        in_specs=placed,
        out_specs=(P(("groups", "col"), "row"), P(("groups", "row"), "col")),
        check_vma=False,
    )
```
